32 devices in a mesh: tok: 4 (over z), con: 4 (over x, core), out: 2 (over y).
Axes of the slice: x: 2, y: 2, z: 4, core: 2. Of those that a mesh axis runs over, the one named last changes fastest.
Arguments:
- tokens: bfloat16 [1024, 10240], P('tok', 'con'), may hold values from -6 to 6
- out_grad: bfloat16 [1024, 10240], P('tok', 'con'), may hold values from -3 to 3
- weight_in: bfloat16 [10240, 20480], P('con', ('tok', 'out')), may hold values from -0.0625 to 0.0625
- weight_out: bfloat16 [20480, 10240], P(('tok', 'out'), 'con'), may hold values from -0.0390625 to 0.0390625
Outputs:
- input_grad: bfloat16 [1024, 10240], P(('tok', 'out'), 'con')
- first_grad: float32 [10240, 20480], P('con', ('tok', 'out'))
- second_grad: float32 [20480, 10240], P(('tok', 'out'), 'con')
The draws below stay inside these ranges and needn't reach their ends.
All inputs are finite; a program needn't handle non-finite values.
Results may differ from the reference program's by a relative error of at most 0.0049.
Values may be sent and summed in bfloat16 or wider, within the bound.
A program may use at most 192 MiB of HBM per device.

```python
import jax
import jax.numpy as jnp
from jax import lax

D = 10240
FF = 20480
TOKENS = 1024


def block_levels(key, dims, cuts, least, largest):
    gain, own = 1.0, jax.random.fold_in(key, 6)
    for dim, blocks in cuts:
        steps = jnp.exp(jax.random.uniform(jax.random.fold_in(own, dim), (blocks,), jnp.float32, least / len(cuts), largest / len(cuts)))
        gain = gain * jnp.repeat(steps, dims[dim] // blocks).reshape([-1 if axis == dim else 1 for axis in range(len(dims))])
    return gain


def normal_values(key, shape, spread, most, pieces=(), kind=jnp.bfloat16):
    drawn = spread * jax.random.normal(key, shape, jnp.float32)
    if pieces:
        drawn = drawn * block_levels(key, shape, pieces, -0.22, 0.18)
    return jnp.clip(drawn, -most, most).astype(kind)


def setup_inputs(seed: int = 0) -> dict:
    arg_keys = jax.random.split(jax.random.key(seed), 5)
    tokens = normal_values(arg_keys[0], (TOKENS, D), 1.0, 6.0, ((0, 4), (1, 4)))
    out_grad = normal_values(arg_keys[1], (TOKENS, D), 0.3, 3.0, ((0, 4), (1, 4)))
    weight_in = normal_values(arg_keys[2], (D, FF), D ** -0.5, 0.0625, ((0, 4), (1, 8)))
    weight_out = normal_values(arg_keys[3], (FF, D), FF ** -0.5, 0.0390625, ((0, 8), (1, 4)))
    return {"tokens": tokens, "out_grad": out_grad, "weight_in": weight_in, "weight_out": weight_out}


def gelu_parts(pre, act_grad):
    cdf = 0.5 * (1.0 + jax.scipy.special.erf(pre * 0.7071067811865476))
    density = jnp.exp(-0.5 * pre * pre) * 0.3989422804014327
    activ = (pre * cdf).astype(jnp.bfloat16)
    pre_grad = (act_grad * (cdf + pre * density)).astype(jnp.bfloat16)
    return activ, pre_grad


def reference(tokens, out_grad, weight_in, weight_out):
    pre = jnp.dot(tokens, weight_in, preferred_element_type=jnp.float32)
    act_grad = lax.dot_general(out_grad, weight_out, (((1,), (1,)), ((), ())), preferred_element_type=jnp.float32)
    activ, pre_grad = gelu_parts(pre, act_grad)
    input_grad = lax.dot_general(pre_grad, weight_in, (((1,), (1,)), ((), ())), preferred_element_type=jnp.float32)
    first_grad = lax.dot_general(tokens, pre_grad, (((0,), (0,)), ((), ())), preferred_element_type=jnp.float32)
    second_grad = lax.dot_general(activ, out_grad, (((0,), (0,)), ((), ())), preferred_element_type=jnp.float32)
    return input_grad.astype(jnp.bfloat16), first_grad, second_grad
```

```python
import functools

import jax
import jax.numpy as jnp
from jax import lax
from jax.experimental import pallas as pl
from jax.experimental.pallas import tpu as pltpu
from jax.sharding import PartitionSpec as P


def gelu_parts(pre, act_grad):
    cdf = 0.5 * (1.0 + jax.scipy.special.erf(pre * 0.7071067811865476))
    density = jnp.exp(-0.5 * pre * pre) * 0.3989422804014327
    activ = (pre * cdf).astype(jnp.bfloat16)
    pre_grad = (act_grad * (cdf + pre * density)).astype(jnp.bfloat16)
    return (activ, pre_grad)


def grad_kernel(chunks, width, *refs):
    left, right, out = refs[:chunks], refs[chunks : 2 * chunks], refs[-1]
    total = out.shape[1]
    for start in range(0, total, width):
        acc = None
        for a, b in zip(left, right):
            term = lax.dot_general(
                a[...],
                b[:, start : start + width],
                (((0,), (0,)), ((), ())),
                preferred_element_type=jnp.float32,
            )
            acc = term if acc is None else acc + term
        out[:, start : start + width] = acc


def summed_outer(left, left_from, left_width, right, right_block, right_width):
    chunks, rows = len(left), left[0].shape[0]
    high = 256 if left_width % 256 == 0 else 128
    width = 512 if right_width % 512 == 0 else 128
    first = left_from // high
    return pl.pallas_call(
        functools.partial(grad_kernel, chunks, width),
        grid=(left_width // high,),
        in_specs=[pl.BlockSpec((rows, high), lambda i: (0, first + i))] * chunks
        + [pl.BlockSpec((rows, right_width), lambda i: (0, right_block))] * chunks,
        out_specs=pl.BlockSpec((high, right_width), lambda i: (i, 0)),
        out_shape=jax.ShapeDtypeStruct((left_width, right_width), jnp.float32),
        compiler_params=pltpu.CompilerParams(
            dimension_semantics=("arbitrary",), vmem_limit_bytes=32 * 1024 * 1024
        ),
        cost_estimate=pl.CostEstimate(
            flops=2 * chunks * rows * left_width * right_width,
            bytes_accessed=4 * left_width * right_width
            + 2 * chunks * rows * (left_width + right_width),
            transcendentals=0,
        ),
    )(*left, *right)


def per_device(T, C, O, tokens, out_grad, weight_in, weight_out):
    bf16, f32 = jnp.bfloat16, jnp.float32
    o, c = lax.axis_index("out"), lax.axis_index("con")
    inner = 2 if C % 2 == 0 else 1
    outer = C // inner
    ci, co = c % inner, c // inner

    def shift(a, axis, size, by):
        return lax.ppermute(a, axis, [(i, (i + by) % size) for i in range(size)])

    def shift_inner(a, by):
        return lax.ppermute(
            a, "con", [(i, i // inner * inner + (i % inner + by) % inner) for i in range(C)]
        )

    def shift_outer(a, by):
        return lax.ppermute(
            a, "con", [(i, (i // inner + by) % outer * inner + i % inner) for i in range(C)]
        )

    shard = tokens.shape[0]
    rows = shard // O
    hidden = weight_in.shape[1]

    def part(a, k):
        return lax.dynamic_slice_in_dim(a, (o - k) % O * rows, rows, 0)

    def whole_shard(own):
        return jnp.concatenate([own] + [shift(own, "out", O, k) for k in range(1, O)], axis=0)

    tok_part, grad_part = part(tokens, 0), part(out_grad, 0)
    toks = [jnp.concatenate([part(tokens, k) for k in range(O)], axis=0)]
    grads = [jnp.concatenate([part(out_grad, k) for k in range(O)], axis=0)]
    for _ in range(1, T):
        tok_part = shift(tok_part, "tok", T, 1)
        grad_part = shift(grad_part, "tok", T, 1)
        toks.append(whole_shard(tok_part))
        grads.append(whole_shard(grad_part))

    def con_sum(pre, grad):
        pre = pre.reshape(outer, inner, shard // C, hidden)
        grad = grad.reshape(outer, inner, shard // C, hidden)

        def pick(a, axis, at):
            return lax.dynamic_index_in_dim(a, at, axis, keepdims=False)

        kept = [pick(pre, 1, ci), pick(grad, 1, ci)]
        for k in range(1, inner):
            to = (ci - k) % inner
            kept[0] = kept[0] + shift_inner(pick(pre, 1, to), -k)
            kept[1] = kept[1] + shift_inner(pick(grad, 1, to), -k)
        held = [pick(kept[0], 0, co), pick(kept[1], 0, co)]
        for k in range(1, outer):
            to = (co - k) % outer
            sent = jnp.concatenate([pick(kept[0], 0, to), pick(kept[1], 0, to)], axis=1)
            got = shift_outer(sent.astype(bf16), -k).astype(f32)
            held = [held[0] + got[:, :hidden], held[1] + got[:, hidden:]]
        return held

    both, result = [], None
    for k in range(T):
        pre = jnp.dot(toks[k], weight_in, preferred_element_type=f32)
        grad = lax.dot_general(
            grads[k], weight_out, (((1,), (1,)), ((), ())), preferred_element_type=f32
        )
        share = jnp.concatenate(gelu_parts(*con_sum(pre, grad)), axis=1)
        chunk = lax.all_gather(share, "con", axis=0, tiled=True)
        both.append(chunk)
        back = lax.dot_general(
            chunk[:, hidden:], weight_in, (((1,), (1,)), ((), ())), preferred_element_type=f32
        )
        total = back[:rows]
        for j in range(1, O):
            sent = back[j * rows : (j + 1) * rows].astype(bf16)
            total = total + shift(sent, "out", O, -j).astype(f32)
        if k:
            total = shift(total.astype(bf16), "tok", T, -k).astype(f32)
        result = total if result is None else result + total

    width = tokens.shape[1]
    first_grad = summed_outer(toks, 0, width, both, 1, hidden)
    second_grad = summed_outer(both, 0, hidden, grads, 0, width)
    return (result.astype(bf16), first_grad, second_grad)


def solution(mesh):
    placed = (P("tok", "con"), P("tok", "con"), P("con", ("tok", "out")), P(("tok", "out"), "con"))
    sizes = [mesh.shape[axis] for axis in ("tok", "con", "out")]
    return jax.shard_map(
        functools.partial(per_device, *sizes),
        mesh=mesh,
        in_specs=placed,
        out_specs=(P(("tok", "out"), "con"), P("con", ("tok", "out")), P(("tok", "out"), "con")),
        check_vma=False,
    )
```

```python
import functools

import jax
import jax.numpy as jnp
from jax import lax
from jax.experimental import pallas as pl
from jax.experimental.pallas import tpu as pltpu
from jax.sharding import PartitionSpec as P


def gelu_parts(pre, act_grad):
    cdf = 0.5 * (1.0 + jax.scipy.special.erf(pre * 0.7071067811865476))
    density = jnp.exp(-0.5 * pre * pre) * 0.3989422804014327
    activ = (pre * cdf).astype(jnp.bfloat16)
    pre_grad = (act_grad * (cdf + pre * density)).astype(jnp.bfloat16)
    return (activ, pre_grad)


def grad_kernel(chunks, width, *refs):
    left, right, out = refs[:chunks], refs[chunks : 2 * chunks], refs[-1]
    total = out.shape[1]
    for start in range(0, total, width):
        acc = None
        for a, b in zip(left, right):
            term = lax.dot_general(
                a[...],
                b[:, start : start + width],
                (((0,), (0,)), ((), ())),
                preferred_element_type=jnp.float32,
            )
            acc = term if acc is None else acc + term
        out[:, start : start + width] = acc


def summed_outer(left, left_from, left_width, right, right_block, right_width):
    chunks, rows = len(left), left[0].shape[0]
    high = 256 if left_width % 256 == 0 else 128
    width = 512 if right_width % 512 == 0 else 128
    first = left_from // high
    return pl.pallas_call(
        functools.partial(grad_kernel, chunks, width),
        grid=(left_width // high,),
        in_specs=[pl.BlockSpec((rows, high), lambda i: (0, first + i))] * chunks
        + [pl.BlockSpec((rows, right_width), lambda i: (0, right_block))] * chunks,
        out_specs=pl.BlockSpec((high, right_width), lambda i: (i, 0)),
        out_shape=jax.ShapeDtypeStruct((left_width, right_width), jnp.float32),
        compiler_params=pltpu.CompilerParams(
            dimension_semantics=("arbitrary",), vmem_limit_bytes=32 * 1024 * 1024
        ),
        cost_estimate=pl.CostEstimate(
            flops=2 * chunks * rows * left_width * right_width,
            bytes_accessed=4 * left_width * right_width
            + 2 * chunks * rows * (left_width + right_width),
            transcendentals=0,
        ),
    )(*left, *right)


def per_device(T, C, O, tokens, out_grad, weight_in, weight_out):
    bf16, f32 = jnp.bfloat16, jnp.float32
    o, c = lax.axis_index("out"), lax.axis_index("con")
    inner = 2 if C % 2 == 0 else 1
    outer = C // inner
    ci, co = c % inner, c // inner

    def shift(a, axis, size, by):
        return lax.ppermute(a, axis, [(i, (i + by) % size) for i in range(size)])

    def shift_inner(a, by):
        return lax.ppermute(
            a, "con", [(i, i // inner * inner + (i % inner + by) % inner) for i in range(C)]
        )

    def shift_outer(a, by):
        return lax.ppermute(
            a, "con", [(i, (i // inner + by) % outer * inner + i % inner) for i in range(C)]
        )

    shard = tokens.shape[0]
    rows = shard // O
    hidden = weight_in.shape[1]

    def part(a, k):
        return lax.dynamic_slice_in_dim(a, (o - k) % O * rows, rows, 0)

    def whole_shard(own):
        return jnp.concatenate([own] + [shift(own, "out", O, k) for k in range(1, O)], axis=0)

    tok_part, grad_part = part(tokens, 0), part(out_grad, 0)
    toks = [jnp.concatenate([part(tokens, k) for k in range(O)], axis=0)]
    grads = [jnp.concatenate([part(out_grad, k) for k in range(O)], axis=0)]
    for _ in range(1, T):
        tok_part = shift(tok_part, "tok", T, 1)
        grad_part = shift(grad_part, "tok", T, 1)
        toks.append(whole_shard(tok_part))
        grads.append(whole_shard(grad_part))

    def con_sum(pre, grad):
        pre = pre.reshape(outer, inner, shard // C, hidden)
        grad = grad.reshape(outer, inner, shard // C, hidden)

        def pick(a, axis, at):
            return lax.dynamic_index_in_dim(a, at, axis, keepdims=False)

        kept = [pick(pre, 1, ci), pick(grad, 1, ci)]
        for k in range(1, inner):
            to = (ci - k) % inner
            kept[0] = kept[0] + shift_inner(pick(pre, 1, to), -k)
            kept[1] = kept[1] + shift_inner(pick(grad, 1, to), -k)
        held = [pick(kept[0], 0, co), pick(kept[1], 0, co)]
        for k in range(1, outer):
            to = (co - k) % outer
            sent = jnp.concatenate([pick(kept[0], 0, to), pick(kept[1], 0, to)], axis=1)
            got = shift_outer(sent.astype(bf16), -k).astype(f32)
            held = [held[0] + got[:, :hidden], held[1] + got[:, hidden:]]
        return held

    def in_order(blocks, at):
        n = len(blocks)
        ordered = []
        for j in range(n):
            k, block = (j - at) % n, blocks[0]
            for other in range(1, n):
                block = jnp.where(k == other, blocks[other], block)
            ordered.append(block)
        return ordered

    def con_gather(share):
        blocks = [share] + [shift_outer(share, -k) for k in range(1, outer)]
        held = jnp.concatenate(in_order(blocks, co), axis=0)
        halves = [held] + [shift_inner(held, -k) for k in range(1, inner)]
        halves = [a.reshape(outer, 1, shard // C, -1) for a in in_order(halves, ci)]
        return jnp.concatenate(halves, axis=1).reshape(shard, -1)

    both, result = [], None
    for k in range(T):
        pre = jnp.dot(toks[k], weight_in, preferred_element_type=f32)
        grad = lax.dot_general(
            grads[k], weight_out, (((1,), (1,)), ((), ())), preferred_element_type=f32
        )
        share = jnp.concatenate(gelu_parts(*con_sum(pre, grad)), axis=1)
        chunk = con_gather(share)
        both.append(chunk)
        back = lax.dot_general(
            chunk[:, hidden:], weight_in, (((1,), (1,)), ((), ())), preferred_element_type=f32
        )
        total = back[:rows]
        for j in range(1, O):
            sent = back[j * rows : (j + 1) * rows].astype(bf16)
            total = total + shift(sent, "out", O, -j).astype(f32)
        if k:
            total = shift(total.astype(bf16), "tok", T, -k).astype(f32)
        result = total if result is None else result + total

    width = tokens.shape[1]
    first_grad = summed_outer(toks, 0, width, both, 1, hidden)
    second_grad = summed_outer(both, 0, hidden, grads, 0, width)
    return (result.astype(bf16), first_grad, second_grad)


def solution(mesh):
    placed = (P("tok", "con"), P("tok", "con"), P("con", ("tok", "out")), P(("tok", "out"), "con"))
    sizes = [mesh.shape[axis] for axis in ("tok", "con", "out")]
    return jax.shard_map(
        functools.partial(per_device, *sizes),
        mesh=mesh,
        in_specs=placed,
        out_specs=(P(("tok", "out"), "con"), P("con", ("tok", "out")), P(("tok", "out"), "con")),
        check_vma=False,
    )
```

```python
import functools

import jax
import jax.numpy as jnp
from jax import lax
from jax.experimental import pallas as pl
from jax.experimental.pallas import tpu as pltpu
from jax.sharding import PartitionSpec as P


def gelu_parts(pre, act_grad):
    cdf = 0.5 * (1.0 + jax.scipy.special.erf(pre * 0.7071067811865476))
    density = jnp.exp(-0.5 * pre * pre) * 0.3989422804014327
    activ = (pre * cdf).astype(jnp.bfloat16)
    pre_grad = (act_grad * (cdf + pre * density)).astype(jnp.bfloat16)
    return (activ, pre_grad)


def grad_kernel(chunks, width, *refs):
    left, right, out = refs[:chunks], refs[chunks : 2 * chunks], refs[-1]
    total = out.shape[1]
    for start in range(0, total, width):
        acc = None
        for a, b in zip(left, right):
            term = lax.dot_general(
                a[...],
                b[:, start : start + width],
                (((0,), (0,)), ((), ())),
                preferred_element_type=jnp.float32,
            )
            acc = term if acc is None else acc + term
        out[:, start : start + width] = acc


def summed_outer(left, left_from, left_width, right, right_block, right_width):
    chunks, rows = len(left), left[0].shape[0]
    high = 256 if left_width % 256 == 0 else 128
    width = 512 if right_width % 512 == 0 else 128
    first = left_from // high
    return pl.pallas_call(
        functools.partial(grad_kernel, chunks, width),
        grid=(left_width // high,),
        in_specs=[pl.BlockSpec((rows, high), lambda i: (0, first + i))] * chunks
        + [pl.BlockSpec((rows, right_width), lambda i: (0, right_block))] * chunks,
        out_specs=pl.BlockSpec((high, right_width), lambda i: (i, 0)),
        out_shape=jax.ShapeDtypeStruct((left_width, right_width), jnp.float32),
        compiler_params=pltpu.CompilerParams(
            dimension_semantics=("arbitrary",), vmem_limit_bytes=32 * 1024 * 1024
        ),
        cost_estimate=pl.CostEstimate(
            flops=2 * chunks * rows * left_width * right_width,
            bytes_accessed=4 * left_width * right_width
            + 2 * chunks * rows * (left_width + right_width),
            transcendentals=0,
        ),
    )(*left, *right)


def per_device(T, C, O, tokens, out_grad, weight_in, weight_out):
    bf16, f32 = jnp.bfloat16, jnp.float32
    o, c = lax.axis_index("out"), lax.axis_index("con")
    inner = 2 if C % 2 == 0 else 1
    outer = C // inner
    ci, co = c % inner, c // inner

    def shift(a, axis, size, by):
        return lax.ppermute(a, axis, [(i, (i + by) % size) for i in range(size)])

    def shift_inner(a, by):
        return lax.ppermute(
            a, "con", [(i, i // inner * inner + (i % inner + by) % inner) for i in range(C)]
        )

    def shift_outer(a, by):
        return lax.ppermute(
            a, "con", [(i, (i // inner + by) % outer * inner + i % inner) for i in range(C)]
        )

    shard = tokens.shape[0]
    rows = shard // O
    hidden = weight_in.shape[1]

    def part(a, k):
        return lax.dynamic_slice_in_dim(a, (o - k) % O * rows, rows, 0)

    def whole_shard(own):
        return jnp.concatenate([own] + [shift(own, "out", O, k) for k in range(1, O)], axis=0)

    tok_part, grad_part = part(tokens, 0), part(out_grad, 0)
    toks = [jnp.concatenate([part(tokens, k) for k in range(O)], axis=0)]
    grads = [jnp.concatenate([part(out_grad, k) for k in range(O)], axis=0)]
    for _ in range(1, T):
        tok_part = shift(tok_part, "tok", T, 1)
        grad_part = shift(grad_part, "tok", T, 1)
        toks.append(whole_shard(tok_part))
        grads.append(whole_shard(grad_part))

    def con_sum(pre, grad):
        pre = pre.reshape(outer, inner, shard // C, hidden)
        grad = grad.reshape(outer, inner, shard // C, hidden)

        def pick(a, axis, at):
            return lax.dynamic_index_in_dim(a, at, axis, keepdims=False)

        kept = [pick(pre, 1, ci), pick(grad, 1, ci)]
        for k in range(1, inner):
            to = (ci - k) % inner
            kept[0] = kept[0] + shift_inner(pick(pre, 1, to), -k)
            kept[1] = kept[1] + shift_inner(pick(grad, 1, to), -k)
        held = [pick(kept[0], 0, co), pick(kept[1], 0, co)]
        for k in range(1, outer):
            to = (co - k) % outer
            sent = jnp.concatenate([pick(kept[0], 0, to), pick(kept[1], 0, to)], axis=1)
            got = shift_outer(sent.astype(bf16), -k).astype(f32)
            held = [held[0] + got[:, :hidden], held[1] + got[:, hidden:]]
        return held

    def in_order(blocks, at):
        n = len(blocks)
        ordered = []
        for j in range(n):
            k, block = (j - at) % n, blocks[0]
            for other in range(1, n):
                block = jnp.where(k == other, blocks[other], block)
            ordered.append(block)
        return ordered

    def con_gather(share):
        blocks = [share] + [shift_outer(share, -k) for k in range(1, outer)]
        held = jnp.concatenate(in_order(blocks, co), axis=0)
        halves = [held] + [shift_inner(held, -k) for k in range(1, inner)]
        halves = [a.reshape(outer, 1, shard // C, -1) for a in in_order(halves, ci)]
        return jnp.concatenate(halves, axis=1).reshape(shard, -1)

    shares, both, result = [], [], None
    for k in range(T):
        tok = toks[k]
        if k >= 2:
            tok, shares[k - 2] = lax.optimization_barrier((tok, shares[k - 2]))
        pre = jnp.dot(tok, weight_in, preferred_element_type=f32)
        grad = lax.dot_general(
            grads[k], weight_out, (((1,), (1,)), ((), ())), preferred_element_type=f32
        )
        shares.append(jnp.concatenate(gelu_parts(*con_sum(pre, grad)), axis=1))
    for k in range(T):
        if k < T - 1:
            chunk = lax.all_gather(shares[k], "con", axis=0, tiled=True)
        else:
            chunk = con_gather(shares[k])
        both.append(chunk)
        back = lax.dot_general(
            chunk[:, hidden:], weight_in, (((1,), (1,)), ((), ())), preferred_element_type=f32
        )
        total = back[:rows]
        for j in range(1, O):
            sent = back[j * rows : (j + 1) * rows].astype(bf16)
            total = total + shift(sent, "out", O, -j).astype(f32)
        if k:
            total = shift(total.astype(bf16), "tok", T, -k).astype(f32)
        result = total if result is None else result + total

    width = tokens.shape[1]
    first_grad = summed_outer(toks, 0, width, both, 1, hidden)
    second_grad = summed_outer(both, 0, hidden, grads, 0, width)
    return (result.astype(bf16), first_grad, second_grad)


def solution(mesh):
    placed = (P("tok", "con"), P("tok", "con"), P("con", ("tok", "out")), P(("tok", "out"), "con"))
    sizes = [mesh.shape[axis] for axis in ("tok", "con", "out")]
    return jax.shard_map(
        functools.partial(per_device, *sizes),
        mesh=mesh,
        in_specs=placed,
        out_specs=(P(("tok", "out"), "con"), P("con", ("tok", "out")), P(("tok", "out"), "con")),
        check_vma=False,
    )
```
